512 devices in a mesh: fsdp: 64 (over z, y_lo, core), tensor: 8 (over y_hi, x).
Axes of the slice: x: 4, y: 8 (y_hi: 2, y_lo: 4; y = y_hi * 4 + y_lo), z: 8, core: 2. Of those that a mesh axis runs over, the one named last changes fastest.
Arguments:
- grad: float32 [512, 16384], P('tensor', 'fsdp'), may hold values from -16 to 16
- basis: float32 [16384, 16384], P('fsdp', 'tensor'), may hold values from -0.046875 to 0.046875
- first_moment: float32 [512, 16384], P('fsdp', 'tensor'), may hold values from -6 to 6
- second_moment: float32 [512, 16384], P('fsdp', 'tensor'), may hold values from 0.25 to 4
Outputs:
- update: float32 [512, 16384], P('tensor', 'fsdp')
- new_first: float32 [512, 16384], P('fsdp', 'tensor')
- new_second: float32 [512, 16384], P('fsdp', 'tensor')
The draws below stay inside these ranges and needn't reach their ends.
All inputs are finite; a program needn't handle non-finite values.
Results may differ from the reference program's by a relative error of at most 0.000076.
Values sent between devices are 32-bit elements; how exact they have to be, the bound alone decides.
A program may use at most 64 MiB of HBM per device.

```python
import math
import jax
import jax.numpy as jnp
from jax import lax

C = 16384
STEP = 10
ROWS = 512


def raised(values, own_key, source, target, parts, factor):
    owner, partner = [(jnp.arange(values.shape[axis_at]) // (values.shape[axis_at] // parts)).reshape([-1 if axis == axis_at else 1 for axis in range(values.ndim)]) for axis_at in (source, target)]
    chosen = jax.random.permutation(own_key, parts)[partner]
    strong = (owner == chosen) | (owner == (partner + parts // 2) % parts)
    return jnp.where(strong, factor * values, values)


def level_of(own_key, dims, cuts, least, largest):
    def one(axis_at, shards_of):
        steps = jax.random.uniform(jax.random.fold_in(jax.random.fold_in(own_key, 6), axis_at), (shards_of,), jnp.float32, least / len(cuts), largest / len(cuts))
        return jnp.repeat(jnp.exp(steps), dims[axis_at] // shards_of).reshape((-1,) + (1,) * (len(dims) - axis_at - 1))

    loudness = one(*cuts[0])
    for cut in cuts[1:]:
        loudness = loudness * one(*cut)
    return loudness


def scatter_about(rng, dims, scale, limit, cuts=(), dtype=jnp.bfloat16):
    level = level_of(rng, dims, cuts, -0.22, 0.18) if cuts else 1.0
    drawn = jax.random.normal(rng, dims, jnp.float32) * scale * level
    return jnp.minimum(jnp.maximum(drawn, -limit), limit).astype(dtype)


def noise_with(own_key, extent, scale, bound, shards, heavy, kind=jnp.bfloat16):
    values = scale * jax.random.normal(own_key, extent, jnp.float32)
    if shards:
        values = values * level_of(own_key, extent, shards, -0.22, 0.18)
    return jnp.clip(raised(values, jax.random.fold_in(own_key, 3), *heavy), -bound, bound).astype(kind)


def setup_inputs(seed: int = 0) -> dict:
    splits = jax.random.split(jax.random.key(seed), 5)
    grad = noise_with(splits[0], (ROWS, C), 1.0, 16.0, ((0, 8), (1, 64)), (1, 0, 64, 4.0), jnp.float32)
    basis = scatter_about(splits[1], (C, C), C ** -0.5, 0.046875, ((0, 64), (1, 8)), jnp.float32)
    first_moment = scatter_about(splits[2], (ROWS, C), 1.0, 6.0, ((0, 64), (1, 8)), jnp.float32)
    second_moment = jnp.clip(jnp.exp(math.log(4.0) - 2.7725887 * jax.random.uniform(splits[3], (ROWS, C), jnp.float32) ** level_of(splits[3], (ROWS, C), ((0, 64), (1, 8)), -0.2, 0.2)), 0.25, 4.0)
    return dict(grad=grad, basis=basis, first_moment=first_moment, second_moment=second_moment)


def moment_step(rotated, first_moment, second_moment):
    new_first = 0.9 * first_moment + 0.1 * rotated
    new_second = 0.95 * second_moment + 0.05 * rotated * rotated
    first_fix = 1.0 - 0.9 ** STEP
    second_fix = 1.0 - 0.95 ** STEP
    direction = new_first / first_fix / (jnp.sqrt(new_second / second_fix) + 1e-08)
    return (new_first, new_second, direction)

def reference(grad, basis, first_moment, second_moment):
    rotated = jnp.dot(grad, basis, precision=lax.Precision.HIGHEST, preferred_element_type=jnp.float32)
    new_first, new_second, direction = moment_step(rotated, first_moment, second_moment)
    update = jnp.dot(direction, basis.T, precision=lax.Precision.HIGHEST, preferred_element_type=jnp.float32)
    return (update, new_first, new_second)
```

```python
import jax
import jax.numpy as jnp
from jax import lax
from jax.experimental import pallas as pl
from jax.experimental.pallas import tpu as pltpu
from jax.sharding import PartitionSpec as P

MESH = pl.DeviceIdType.MESH
F32, BF16 = jnp.float32, jnp.bfloat16
STEP = 10
C = 2048
K = 256
WA = 1536
WB = C - WA
HA, HB = WA // 2, WB // 2


def moment_step(rotated, first_moment, second_moment):
    new_first = 0.9 * first_moment + 0.1 * rotated
    new_second = 0.95 * second_moment + 0.05 * rotated * rotated
    first_fix = 1.0 - 0.9**STEP
    second_fix = 1.0 - 0.95**STEP
    direction = new_first / first_fix / (jnp.sqrt(new_second / second_fix) + 1e-08)
    return (new_first, new_second, direction)


def halves(x):
    hi = x.astype(BF16)
    return hi, (x - hi.astype(F32)).astype(BF16)


def kernel(
    grad, basis, m1, m2,
    update, nf, ns,
    own, sib, bhi, blo, g, ast, pf, ra, ya, yb, rb, d, u, xr, st, fin,
    local_sem, send, basis_sem, g_sem, ra_sem, ya_sem, yb_sem, rb_sem,
    da_sem, dya_sem, db_sem, dyb_sem, x_sem, fin_sem,
):
    f, t = lax.axis_index("fsdp"), lax.axis_index("tensor")
    z, yl, c = f // 8, (f // 2) % 4, f % 2
    yh, x = t // 4, t % 4

    def dev(dx=0, dh=0, dl=0, dz=0, dc=0):
        return (
            ((z + dz + 8) % 8) * 8 + ((yl + dl + 4) % 4) * 2 + (c + dc) % 2,
            ((yh + dh) % 2) * 4 + (x + dx + 4) % 4,
        )

    barrier = pltpu.get_barrier_semaphore()
    friends = [dev(dc=1), dev(dz=1), dev(dz=-1)]
    friends += [dev(dl=j) for j in (1, 2, 3)]
    friends += [dev(dh=1, dc=e) for e in (0, 1)]
    friends += [dev(dx=j, dc=e) for j in (1, 2, 3) for e in (0, 1)]
    for friend in friends:
        pl.semaphore_signal(barrier, inc=1, device_id=friend, device_id_type=MESH)
    load = pltpu.make_async_copy(basis, own, local_sem)
    load.start()

    started = []

    def remote(src, dst, recv_sem, to):
        return pltpu.make_async_remote_copy(
            src_ref=src, dst_ref=dst, send_sem=send.at[len(started)],
            recv_sem=recv_sem, device_id=to, device_id_type=MESH,
        )

    def put(src, dst, recv_sem, to):
        copy = remote(src, dst, recv_sem, to)
        copy.start()
        started.append(copy)

    def got(dst, recv_sem):
        pltpu.make_async_remote_copy(
            src_ref=dst, dst_ref=dst, send_sem=send.at[0],
            recv_sem=recv_sem, device_id=dev(dc=1), device_id_type=MESH,
        ).wait_recv()

    def split_basis(src, base):
        @pl.loop(0, K // 16)
        def _(i):
            hi, lo = halves(src[pl.ds(pl.multiple_of(i * 16, 16), 16), :])
            at = pl.multiple_of(base + i * 16, 16)
            bhi[pl.ds(at, 16), :] = hi
            blo[pl.ds(at, 16), :] = lo

    g[t, 0] = grad[:, c]
    load.wait()
    split_basis(own, 0)
    pl.semaphore_wait(barrier, len(friends))

    tp = ((yh + 1) % 2) * 4 + x
    for e in (0, 1):
        put(grad.at[:, (c + e) % 2], g.at[t, e], g_sem.at[1, e], dev(dh=1, dc=e))
    put(grad.at[:, 1 - c], g.at[t, 1], g_sem.at[0, 1], dev(dc=1))
    for j in (1, 3, 2):
        for e in (0, 1):
            put(grad.at[:, (c + e) % 2], g.at[t, e], g_sem.at[1 + j, e], dev(dx=j, dc=e))
    put(own, sib, basis_sem, dev(dc=1))
    for e in (0, 1):
        got(g.at[tp, e], g_sem.at[1, e])
    for j in (1, 3, 2):
        put(g.at[tp], g.at[tp], g_sem.at[4 + j, 0], dev(dx=j))
    got(sib, basis_sem)
    split_basis(sib, K)
    got(g.at[t, 1], g_sem.at[0, 1])
    for j in (1, 3, 2):
        for e in (0, 1):
            got(g.at[yh * 4 + (x + 4 - j) % 4, e], g_sem.at[1 + j, e])
    for j in (1, 3, 2):
        got(g.at[((yh + 1) % 2) * 4 + (x + 4 - j) % 4], g_sem.at[4 + j, 0])

    for e in (0, 1):
        hi, lo = halves(g[:, e].reshape(256, K))
        ast[0:256, e * K : (e + 1) * K] = hi
        ast[256:512, e * K : (e + 1) * K] = lo

    def front(i):
        cols = pl.ds(pl.multiple_of(i * 512, 512), 512)
        big = jnp.dot(ast[...], bhi[:, cols], preferred_element_type=F32)
        out = big[0:256] + big[256:512]
        out += jnp.dot(ast[0:256, :], blo[:, cols], preferred_element_type=F32)
        pf[:, :, :, cols] = out.reshape(8, 4, 8, 512)

    front(3)
    for j in (1, 2, 3):
        put(
            pf.at[:, (yl + j) % 4, :, pl.ds(WA, WB)], yb.at[j - 1],
            yb_sem.at[j - 1], dev(dl=j),
        )

    @pl.loop(0, WA // 512)
    def _(i):
        front(i)

    SIGN = (1, -1)
    order = (1, 2, 3, 0)

    def zed(k):
        return (z + k + 16) % 8

    def cut(base, half, way, s):
        return pl.ds(base + way * half, half) if s == 0 else pl.ds(base, 2 * half)

    def send_a(s, j, way):
        q, cols = (yl + j) % 4, cut(0, HA, way, s)
        put(
            pf.at[zed(SIGN[way] * (4 - s)), q, :, cols], ra.at[way, s, j, :, cols],
            ra_sem.at[way, s, j], dev(dz=SIGN[way]),
        )

    def send_b(s, way):
        put(
            pf.at[zed(SIGN[way] * (4 - s)), yl, :, cut(WA, HB, way, s)],
            rb.at[way, s, :, cut(0, HB, way, s)],
            rb_sem.at[way, s], dev(dz=SIGN[way]),
        )

    def add_a(s, j, way):
        q, cols = (yl + j) % 4, cut(0, HA, way, s)
        got(ra.at[way, s, j, :, cols], ra_sem.at[way, s, j])
        at = zed(SIGN[way] * (3 - s))
        pf[at, q, :, cols] = pf[at, q, :, cols] + ra[way, s, j, :, cols]

    def add_b(s, way):
        cols = cut(0, HB, way, s)
        got(rb.at[way, s, :, cols], rb_sem.at[way, s])
        at, to = zed(SIGN[way] * (3 - s)), cut(WA, HB, way, s)
        pf[at, yl, :, to] = pf[at, yl, :, to] + rb[way, s, :, cols]

    def step_a(s, j):
        for way in (0, 1):
            add_a(s, j, way)
            send_a(s + 1, j, way)

    def step_b(s):
        for way in (0, 1):
            add_b(s, way)
            if s < 3:
                send_b(s + 1, way)

    def last_a(j):
        for way in (0, 1):
            add_a(3, j, way)
        if j:
            put(
                pf.at[z, (yl + j) % 4, :, pl.ds(0, WA)], ya.at[j - 1],
                ya_sem.at[j - 1], dev(dl=j),
            )

    for j in order:
        for way in (0, 1):
            send_a(0, j, way)
    for s in (0, 1):
        for j in order:
            step_a(s, j)
    for j in (1, 2, 3):
        got(yb.at[j - 1], yb_sem.at[j - 1])
    bcols = pl.ds(WA, WB)
    pf[:, yl, :, bcols] = pf[:, yl, :, bcols] + yb[0] + yb[1] + yb[2]
    for way in (0, 1):
        send_b(0, way)
    step_a(2, 1)
    step_a(2, 2)
    step_b(0)
    step_a(2, 3)
    step_a(2, 0)
    step_b(1)
    last_a(1)
    last_a(2)
    step_b(2)
    last_a(3)
    step_b(3)

    def moments(rotated, base, width):
        cols = pl.ds(base, width)
        a, b, direction = moment_step(rotated, m1[:, cols], m2[:, cols])
        nf[:, cols] = a
        ns[:, cols] = b
        d[z, yl, :, cols] = direction

    def fwd_a(s, j, way):
        at, q = zed(-SIGN[way] * s), (yl + 4 - j) % 4
        cols = pl.ds(way * HA, HA) if s == 3 else pl.ds(0, WA)
        if s:
            got(d.at[at, q, :, pl.ds(0, WA)], da_sem.at[way, s - 1, j])
        put(
            d.at[at, q, :, cols], d.at[at, q, :, cols],
            da_sem.at[way, s, j], dev(dz=SIGN[way]),
        )

    def spread_b(k, n):
        at = zed(k)
        for j in (1, 2, 3):
            put(
                d.at[at, yl, :, bcols], d.at[at, yl, :, bcols],
                dyb_sem.at[n, j - 1], dev(dl=j),
            )

    def fwd_b(s):
        for way in (0, 1):
            at = zed(-SIGN[way] * s)
            cols = pl.ds(WA + way * HB, HB) if s == 3 else bcols
            if s:
                got(d.at[at, yl, :, bcols], db_sem.at[way, s - 1])
            put(
                d.at[at, yl, :, cols], d.at[at, yl, :, cols],
                db_sem.at[way, s], dev(dz=SIGN[way]),
            )
        if s:
            for way in (0, 1):
                spread_b(-SIGN[way] * s, 2 * s - 1 + way)
        else:
            spread_b(0, 0)

    moments(pf[z, yl, :, bcols], WA, WB)
    fwd_b(0)
    last_a(0)
    for j in (1, 2, 3):
        got(ya.at[j - 1], ya_sem.at[j - 1])
    moments(pf[z, yl, :, pl.ds(0, WA)] + ya[0] + ya[1] + ya[2], 0, WA)
    acols = pl.ds(0, WA)
    for way in (0, 1):
        fwd_a(0, 0, way)
    for j in (1, 2, 3):
        put(
            d.at[z, yl, :, acols], d.at[z, yl, :, acols],
            dya_sem.at[j - 1], dev(dl=j),
        )
    for j in (1, 2, 3):
        got(d.at[z, (yl + 4 - j) % 4, :, acols], dya_sem.at[j - 1])
        for way in (0, 1):
            fwd_a(0, j, way)
        if j == 1:
            fwd_b(1)
    fwd_b(2)

    def wait_b(k, n):
        for j in (1, 2, 3):
            got(d.at[zed(k), (yl + 4 - j) % 4, :, bcols], dyb_sem.at[n, j - 1])

    cond_sends = []

    def flush(n0):
        for copy, pred in cond_sends[n0:]:
            @pl.when(pred)
            def _():
                copy.start()

    def finish(k):
        tt = zed(k)
        hh = tt // 4

        @pl.when(tt % 4 == x)
        def _():
            for j in (1, 2, 3):
                got(xr.at[hh, j - 1], x_sem.at[hh, j - 1])
            total = u[tt] + xr[hh, 0] + xr[hh, 1] + xr[hh, 2]
            for e in (0, 1):
                st[hh, e] = total[:, e * K : (e + 1) * K]

            @pl.when(hh == yh)
            def _():
                final[0].start()

            @pl.when(hh != yh)
            def _():
                final[1].start()
                final[2].start()

    NS = 160
    other = (yh + 1) % 2

    def final_copy(i, src, to):
        return pltpu.make_async_remote_copy(
            src_ref=src, dst_ref=fin.at[i], send_sem=send.at[NS - 1 - i],
            recv_sem=fin_sem.at[i], device_id=to, device_id_type=MESH,
        )

    final = [
        final_copy(0, st.at[yh, 1], dev(dc=1)),
        final_copy(1, st.at[other, 0], dev(dh=1)),
        final_copy(2, st.at[other, 1], dev(dh=1, dc=1)),
    ]
    SB = 144

    def back(ks):
        n0 = len(cond_sends)
        rows = 32 * len(ks)
        parts = [d[zed(k)].reshape(32, C) for k in ks]
        hi, lo = halves(jnp.concatenate(parts, 0) if len(ks) > 1 else parts[0])
        nt = (((1,), (1,)), ((), ()))
        big = lax.dot_general(
            jnp.concatenate([hi, lo], 0), bhi[...], nt, preferred_element_type=F32
        )
        out = big[0:rows] + big[rows : 2 * rows]
        out += lax.dot_general(hi, blo[...], nt, preferred_element_type=F32)
        for i, k in enumerate(ks):
            u[zed(k)] = out[32 * i : 32 * i + 32]
        for k in ks:
            tt = zed(k)
            xx, hh = tt % 4, tt // 4
            slot = (xx + 3 - x + 4) % 4
            slot = jnp.minimum(slot, 2)
            copy = pltpu.make_async_remote_copy(
                src_ref=u.at[tt], dst_ref=xr.at[hh, slot],
                send_sem=send.at[SB + len(cond_sends)],
                recv_sem=x_sem.at[hh, slot],
                device_id=(f, yh * 4 + xx), device_id_type=MESH,
            )
            cond_sends.append((copy, xx != x))
        flush(n0)

    for j in (0, 1):
        for way in (0, 1):
            fwd_a(1, j, way)
    fwd_b(3)
    for j in (2, 3):
        for way in (0, 1):
            fwd_a(1, j, way)
    for way in (0, 1):
        half = pl.ds(WA + way * HB, HB)
        got(d.at[zed(4), yl, :, half], db_sem.at[way, 3])
    spread_b(4, 7)
    wait_b(0, 0)
    back([0])
    for j in range(4):
        for way in (0, 1):
            fwd_a(2, j, way)
    for way in (0, 1):
        wait_b(-SIGN[way], 1 + way)
    back([1, -1])
    finish(0)
    for j in range(4):
        for way in (0, 1):
            fwd_a(3, j, way)
    for way in (0, 1):
        wait_b(-SIGN[way] * 2, 3 + way)
    back([2, -2])
    finish(1)
    finish(-1)
    for way in (0, 1):
        wait_b(-SIGN[way] * 3, 5 + way)
    back([3, -3])
    finish(2)
    finish(-2)
    for j in range(4):
        for way in (0, 1):
            got(
                d.at[zed(4), (yl + 4 - j) % 4, :, pl.ds(way * HA, HA)],
                da_sem.at[way, 3, j],
            )
    wait_b(4, 7)
    back([4])
    finish(3)
    finish(-3)
    finish(4)

    for i in range(3):
        got(fin.at[i], fin_sem.at[i])
    update[:, c] = (st[yh, 0] + fin[1]).reshape(4, 8, K)
    update[:, 1 - c] = (fin[0] + fin[2]).reshape(4, 8, K)

    assert len(started) <= SB
    for copy in started:
        copy.wait_send()
    for copy, pred in cond_sends:
        @pl.when(pred)
        def _():
            copy.wait_send()
    for copy in final:
        copy.wait_send()


def shards(grad, basis, m1, m2):
    vmem = pl.BlockSpec(memory_space=pltpu.VMEM)
    dma = pltpu.SemaphoreType.DMA
    update, nf, ns = pl.pallas_call(
        kernel,
        out_shape=(
            jax.ShapeDtypeStruct((4, 2, 8, K), F32),
            jax.ShapeDtypeStruct((8, C), F32),
            jax.ShapeDtypeStruct((8, C), F32),
        ),
        in_specs=[vmem, pl.BlockSpec(memory_space=pl.ANY), vmem, vmem],
        out_specs=(vmem, vmem, vmem),
        scratch_shapes=[
            pltpu.VMEM((K, C), F32),
            pltpu.VMEM((K, C), F32),
            pltpu.VMEM((2 * K, C), BF16),
            pltpu.VMEM((2 * K, C), BF16),
            pltpu.VMEM((8, 2, 4, 8, K), F32),
            pltpu.VMEM((512, 2 * K), BF16),
            pltpu.VMEM((8, 4, 8, C), F32),
            pltpu.VMEM((2, 4, 4, 8, WA), F32),
            pltpu.VMEM((3, 8, WA), F32),
            pltpu.VMEM((3, 8, 8, WB), F32),
            pltpu.VMEM((2, 4, 8, WB), F32),
            pltpu.VMEM((8, 4, 8, C), F32),
            pltpu.VMEM((8, 32, 2 * K), F32),
            pltpu.VMEM((2, 3, 32, 2 * K), F32),
            pltpu.VMEM((2, 2, 32, K), F32),
            pltpu.VMEM((3, 32, K), F32),
            dma,
            dma((160,)),
            dma,
            dma((8, 2)),
            dma((2, 4, 4)),
            dma((3,)),
            dma((3,)),
            dma((2, 4)),
            dma((2, 4, 4)),
            dma((3,)),
            dma((2, 4)),
            dma((8, 3)),
            dma((2, 3)),
            dma((3,)),
        ],
        compiler_params=pltpu.CompilerParams(
            collective_id=0, has_side_effects=True, vmem_limit_bytes=48 * 2**20
        ),
        name="soap_step",
    )(grad.reshape(4, 2, 8, K), basis, m1, m2)
    return update.reshape(64, K), nf, ns


def solution(mesh):
    return jax.shard_map(
        shards,
        mesh=mesh,
        in_specs=(
            P("tensor", "fsdp"),
            P("fsdp", "tensor"),
            P("fsdp", "tensor"),
            P("fsdp", "tensor"),
        ),
        out_specs=(P("tensor", "fsdp"), P("fsdp", "tensor"), P("fsdp", "tensor")),
        check_vma=False,
    )
```

```python
import jax
import jax.numpy as jnp
from jax import lax
from jax.experimental import pallas as pl
from jax.experimental.pallas import tpu as pltpu
from jax.sharding import PartitionSpec as P

MESH = pl.DeviceIdType.MESH
F32, BF16 = jnp.float32, jnp.bfloat16
STEP = 10
C = 2048
K = 256
PARTS = ((0, 768), (768, 768))
WA = PARTS[1][0] + PARTS[1][1]
WB = C - WA
FAR = (4, 3, -3, 2, -2, 1, -1)
SB = 200


def moment_step(rotated, first_moment, second_moment):
    new_first = 0.9 * first_moment + 0.1 * rotated
    new_second = 0.95 * second_moment + 0.05 * rotated * rotated
    first_fix = 1.0 - 0.9**STEP
    second_fix = 1.0 - 0.95**STEP
    direction = new_first / first_fix / (jnp.sqrt(new_second / second_fix) + 1e-08)
    return (new_first, new_second, direction)


def halves(x):
    hi = x.astype(BF16)
    return hi, (x - hi.astype(F32)).astype(BF16)


def kernel(
    grad_hbm, basis, m1_hbm, m2_hbm,
    update_hbm, nf_hbm, ns_hbm,
    update, nf, ns, own, sib, bhi, blo, grad, m1, m2, gl, g, ast, pf, ra, ya, yb, rb, d, u, xr, st, fin,
    local_sem, send, basis_sem, g_sem, ra_sem, ya_sem, yb_sem, rb_sem,
    da_sem, dya_sem, db_sem, dyb_sem, x_sem, fin_sem,
):
    f, t = lax.axis_index("fsdp"), lax.axis_index("tensor")
    z, yl, c = f // 8, (f // 2) % 4, f % 2
    yh, x = t // 4, t % 4

    def dev(dx=0, dh=0, dl=0, dz=0, dc=0):
        return (
            ((z + dz + 8) % 8) * 8 + ((yl + dl + 4) % 4) * 2 + (c + dc) % 2,
            ((yh + dh) % 2) * 4 + (x + dx + 4) % 4,
        )

    barrier = pltpu.get_barrier_semaphore()
    friends = [dev(dh=1, dc=e) for e in (0, 1)]
    friends += [dev(dx=j, dc=e) for j in (2, 1, 3) for e in (0, 1)]
    friends += [dev(dl=j) for j in (1, 2, 3)]
    friends += [dev(dz=k) for k in FAR] + [dev(dc=1)]
    for friend in friends:
        pl.semaphore_signal(barrier, inc=1, device_id=friend, device_id_type=MESH)
    loads = [
        pltpu.make_async_copy(a, b, local_sem.at[i])
        for i, (a, b) in enumerate(
            ((grad_hbm, grad), (basis, own), (m1_hbm, m1), (m2_hbm, m2))
        )
    ]
    for copy in loads:
        copy.start()
    outs = [
        pltpu.make_async_copy(a, b, local_sem.at[4 + i])
        for i, (a, b) in enumerate(((update, update_hbm), (nf, nf_hbm), (ns, ns_hbm)))
    ]

    started = []

    def put(src, dst, recv_sem, to):
        copy = pltpu.make_async_remote_copy(
            src_ref=src, dst_ref=dst, send_sem=send.at[len(started)],
            recv_sem=recv_sem, device_id=to, device_id_type=MESH,
        )
        copy.start()
        started.append(copy)

    def got(dst, recv_sem):
        pltpu.make_async_remote_copy(
            src_ref=dst, dst_ref=dst, send_sem=send.at[0],
            recv_sem=recv_sem, device_id=dev(dc=1), device_id_type=MESH,
        ).wait_recv()

    def split_basis(src, base):
        @pl.loop(0, K // 16)
        def _(i):
            hi, lo = halves(src[pl.ds(pl.multiple_of(i * 16, 16), 16), :])
            at = pl.multiple_of(base + i * 16, 16)
            bhi[pl.ds(at, 16), :] = hi
            blo[pl.ds(at, 16), :] = lo

    loads[0].wait()
    for e in (0, 1):
        for j in range(4):
            gl[e, j] = grad[(yl + j) % 4, (c + e) % 2]
    g[t, 0] = gl[0]
    pl.semaphore_wait(barrier, len(friends))

    tp = ((yh + 1) % 2) * 4 + x
    HALF = (pl.ds(0, 2), pl.ds(2, 2))
    for h in (0, 1):
        for e in (0, 1):
            put(gl.at[e, HALF[h]], g.at[t, e, HALF[h]], g_sem.at[1, e, h], dev(dh=1, dc=e))
    for j in (1, 3, 2):
        for e in (0, 1):
            put(gl.at[e], g.at[t, e], g_sem.at[1 + j, e, 0], dev(dx=j, dc=e))
    put(gl.at[1], g.at[t, 1], g_sem.at[0, 1, 0], dev(dc=1))
    put(basis, sib, basis_sem, dev(dc=1))
    loads[1].wait()
    split_basis(own, 0)
    for h in (0, 1):
        for e in (0, 1):
            got(g.at[tp, e, HALF[h]], g_sem.at[1, e, h])
        for j in (1, 3, 2):
            put(
                g.at[tp, :, HALF[h]], g.at[tp, :, HALF[h]],
                g_sem.at[4 + j, 0, h], dev(dx=j),
            )
    got(sib, basis_sem)
    split_basis(sib, K)
    got(g.at[t, 1], g_sem.at[0, 1, 0])
    for j in (1, 3, 2):
        for e in (0, 1):
            got(g.at[yh * 4 + (x + 4 - j) % 4, e], g_sem.at[1 + j, e, 0])

    def split_grad(side):
        first = pl.multiple_of(side * 128, 128)
        for e in (0, 1):
            hi, lo = halves(g[pl.ds(side * 4, 4), e].reshape(128, K))
            ast[pl.ds(first, 128), e * K : (e + 1) * K] = hi
            ast[pl.ds(256 + first, 128), e * K : (e + 1) * K] = lo

    def front(base, width, side=None):
        for at in range(base, base + width, 256):
            step = min(256, base + width - at)
            cols = pl.ds(at, step)
            if side is None:
                hi, both, rows, blocks = ast[0:256, :], ast[...], 256, pl.ds(0, 8)
            else:
                first = pl.multiple_of(side * 128, 128)
                hi = ast[pl.ds(first, 128), :]
                both = jnp.concatenate([hi, ast[pl.ds(256 + first, 128), :]], 0)
                rows, blocks = 128, pl.ds(side * 4, 4)
            big = jnp.dot(both, bhi[:, cols], preferred_element_type=F32)
            out = big[0:rows] + big[rows : 2 * rows]
            out += jnp.dot(hi, blo[:, cols], preferred_element_type=F32)
            pf[blocks, :, :, cols] = out.reshape(rows // 32, 4, 8, step)

    acols = [pl.ds(*PARTS[a]) for a in (0, 1)]
    bcols = pl.ds(WA, WB)

    def front_b(side, n):
        front(WA, WB, side)
        blocks = pl.ds(side * 4, 4)
        for j in (1, 2, 3):
            put(
                pf.at[blocks, j, :, bcols], yb.at[j - 1, blocks],
                yb_sem.at[n, j - 1], dev(dl=j),
            )

    split_grad(yh)
    front_b(yh, 0)
    for h in (0, 1):
        for j in (1, 3, 2):
            got(
                g.at[((yh + 1) % 2) * 4 + (x + 4 - j) % 4, :, HALF[h]],
                g_sem.at[4 + j, 0, h],
            )
    split_grad((yh + 1) % 2)

    SIGN = (1, -1)

    def zed(k):
        return (z + k + 16) % 8

    def send_a(a, s, j, way):
        put(
            pf.at[zed(SIGN[way] * (4 - s)), j, :, acols[a]],
            ra.at[way, s, j, :, acols[a]],
            ra_sem.at[way, a, s, j], dev(dz=SIGN[way]),
        )

    def add_a(a, s, j, way):
        piece = ra.at[way, s, j, :, acols[a]]
        got(piece, ra_sem.at[way, a, s, j])
        at = zed(SIGN[way] * (3 - s))
        pf[at, j, :, acols[a]] = pf[at, j, :, acols[a]] + piece[...]

    def round_a(a, r):
        for j in (2, 3, 1, 0):
            for way in (0, 1):
                s = r if (j >= 2) == (way == 0) else r + 1
                if s >= 1 and r >= 1 and s <= 4:
                    add_a(a, s - 1, j, way)
                if s <= 3:
                    send_a(a, s, j, way)
            if r == 4 and j:
                put(
                    pf.at[z, j, :, acols[a]], ya.at[j - 1, :, acols[a]],
                    ya_sem.at[a, j - 1], dev(dl=j),
                )

    def begin_b():
        for n, side in enumerate((yh, (yh + 1) % 2)):
            for j in (1, 2, 3):
                got(yb.at[j - 1, pl.ds(side * 4, 4)], yb_sem.at[n, j - 1])
        pf[:, 0, :, bcols] = pf[:, 0, :, bcols] + yb[0] + yb[1] + yb[2]
        for i, k in enumerate(FAR):
            put(pf.at[zed(k), 0, :, bcols], rb.at[i], rb_sem.at[i], dev(dz=k))

    def end_b():
        total = pf[z, 0, :, bcols]
        for i in range(7):
            got(rb.at[i], rb_sem.at[i])
            total = total + rb[i]
        moments(total, bcols)
        block = d.at[z, 0, :, bcols]
        for i, k in enumerate(FAR):
            put(block, block, db_sem.at[i], dev(dz=k))
        spread_b(0)

    def moments(rotated, cols):
        a, b, direction = moment_step(rotated, m1[:, cols], m2[:, cols])
        nf[:, cols] = a
        ns[:, cols] = b
        d[z, 0, :, cols] = direction

    def fwd_a(a, s, j):
        for way in (0, 1):
            at = zed(-SIGN[way] * s)
            block = d.at[at, j, :, acols[a]]
            if s:
                got(block, da_sem.at[way, a, s - 1, j])
            if s < 3 or (j < 2) == (way == 0):
                put(block, block, da_sem.at[way, a, s, j], dev(dz=SIGN[way]))

    def begin_a(a):
        for j in (1, 2, 3):
            got(ya.at[j - 1, :, acols[a]], ya_sem.at[a, j - 1])
        moments(
            pf[z, 0, :, acols[a]] + ya[0, :, acols[a]] + ya[1, :, acols[a]]
            + ya[2, :, acols[a]], acols[a],
        )
        for j in (1, 2, 3):
            put(
                d.at[z, 0, :, acols[a]], d.at[z, 4 - j, :, acols[a]],
                dya_sem.at[a, j - 1], dev(dl=j),
            )
        fwd_a(a, 0, 0)

    def gather_a(a, s):
        if s:
            fwd_a(a, s, 0)
        for j in (3, 1, 2):
            if s == 0:
                got(d.at[z, j, :, acols[a]], dya_sem.at[a, 3 - j])
            fwd_a(a, s, j)

    def end_a(a):
        for j in range(4):
            got(d.at[zed(4), j, :, acols[a]], da_sem.at[j // 2, a, 3, j])

    def spread_b(k):
        for j in (1, 2, 3):
            put(
                d.at[zed(k), 0, :, bcols], d.at[zed(k), 4 - j, :, bcols],
                dyb_sem.at[k % 8, j - 1], dev(dl=j),
            )

    def gather_b(*ks):
        for k in ks:
            got(d.at[zed(k), 0, :, bcols], db_sem.at[FAR.index(4 if k == 4 else -k)])
            spread_b(k)

    def wait_b(*ks):
        for k in ks:
            for j in (1, 2, 3):
                got(d.at[zed(k), 4 - j, :, bcols], dyb_sem.at[k % 8, j - 1])

    NT = (((1,), (1,)), ((), ()))

    def product(hi, lo, cols):
        rows = hi.shape[0]
        big = lax.dot_general(
            jnp.concatenate([hi, lo], 0), bhi[:, cols], NT, preferred_element_type=F32
        )
        out = big[0:rows] + big[rows : 2 * rows]
        return out + lax.dot_general(hi, blo[:, cols], NT, preferred_element_type=F32)

    cond_sends = []

    def back(part, ks):
        width = C - PARTS[0][1] if part else PARTS[0][1]
        cols = pl.ds(part * PARTS[0][1], width)
        parts = [d[zed(k), :, :, cols].reshape(32, width) for k in ks]
        out = product(*halves(jnp.concatenate(parts, 0) if len(ks) > 1 else parts[0]), cols)
        for i, k in enumerate(ks):
            mine = out[32 * i : 32 * i + 32]
            u[zed(k)] = u[zed(k)] + mine if part else mine
        if part == 0:
            return
        for k in ks:
            tt = zed(k)
            xx, hh = tt % 4, tt // 4
            slot = jnp.minimum((xx + 7 - x) % 4, 2)
            copy = pltpu.make_async_remote_copy(
                src_ref=u.at[tt], dst_ref=xr.at[hh, slot],
                send_sem=send.at[SB + len(cond_sends)],
                recv_sem=x_sem.at[hh, slot],
                device_id=(f, yh * 4 + xx), device_id_type=MESH,
            )
            cond_sends.append((copy, xx != x))

            @pl.when(xx != x)
            def _():
                copy.start()

    other = (yh + 1) % 2

    def final_copy(i, src, to):
        return pltpu.make_async_remote_copy(
            src_ref=src, dst_ref=fin.at[i], send_sem=send.at[SB + 8 + i],
            recv_sem=fin_sem.at[i], device_id=to, device_id_type=MESH,
        )

    final = [
        final_copy(0, st.at[yh, 1], dev(dc=1)),
        final_copy(1, st.at[other, 0], dev(dh=1)),
        final_copy(2, st.at[other, 1], dev(dh=1, dc=1)),
    ]

    def finish(k):
        tt = zed(k)
        hh = tt // 4

        @pl.when(tt % 4 == x)
        def _():
            for j in (1, 2, 3):
                got(xr.at[hh, j - 1], x_sem.at[hh, j - 1])
            total = u[tt] + xr[hh, 0] + xr[hh, 1] + xr[hh, 2]
            for e in (0, 1):
                st[hh, e] = total[:, e * K : (e + 1) * K]

            @pl.when(hh == yh)
            def _():
                final[0].start()

            @pl.when(hh != yh)
            def _():
                final[1].start()
                final[2].start()

    front(*PARTS[0])
    round_a(0, 0)
    front_b((yh + 1) % 2, 1)
    front(*PARTS[1])
    round_a(1, 0)
    for copy in loads[2:]:
        copy.wait()
    round_a(0, 1)
    round_a(1, 1)
    round_a(0, 2)
    round_a(1, 2)
    round_a(0, 3)
    round_a(1, 3)
    begin_b()
    round_a(0, 4)
    round_a(1, 4)
    begin_a(0)
    begin_a(1)
    end_b()
    gather_a(0,0)
    gather_a(1,0)
    gather_a(0,1)
    gather_b(1,-1)
    gather_b(2,-2)
    gather_a(1,1)
    gather_b(3,-3)
    gather_b(4)
    back(0,[0])
    back(0,[1,-1])
    outs[1].start()
    outs[2].start()
    gather_a(0,2)
    wait_b(0)
    back(1,[0])
    gather_a(1,2)
    back(0,[2,-2])
    wait_b(1,-1)
    back(1,[1,-1])
    gather_a(0, 3)
    gather_a(1, 3)
    finish(0)
    back(0, [3, -3])
    wait_b(2, -2)
    back(1, [2, -2])
    finish(1)
    finish(-1)
    end_a(0)
    back(0, [4])
    wait_b(3, -3)
    back(1, [3, -3])
    finish(2)
    finish(-2)
    end_a(1)
    wait_b(4)
    back(1, [4])
    finish(3)
    finish(-3)
    finish(4)

    for i in range(3):
        got(fin.at[i], fin_sem.at[i])
    mine = st[yh, 0] + fin[1]
    theirs = fin[0] + fin[2]
    for j in range(4):
        update[(yl + j) % 4, c] = mine[8 * j : 8 * j + 8]
        update[(yl + j) % 4, 1 - c] = theirs[8 * j : 8 * j + 8]

    assert len(started) <= SB
    outs[0].start()
    for copy in started:
        copy.wait_send()
    for copy, pred in cond_sends:
        @pl.when(pred)
        def _():
            copy.wait_send()
    for copy in final:
        copy.wait_send()
    for copy in outs:
        copy.wait()


def hand_over(a, b, c, to_a, to_b, to_c):
    to_a[...] = a[...]
    to_b[...] = b[...]
    to_c[...] = c[...]


def shards(grad, basis, m1, m2):
    anywhere = pl.BlockSpec(memory_space=pl.ANY)
    dma = pltpu.SemaphoreType.DMA
    update, nf, ns = pl.pallas_call(
        kernel,
        out_shape=(
            jax.ShapeDtypeStruct((4, 2, 8, K), F32),
            jax.ShapeDtypeStruct((8, C), F32),
            jax.ShapeDtypeStruct((8, C), F32),
        ),
        in_specs=[anywhere] * 4,
        out_specs=(anywhere,) * 3,
        scratch_shapes=[
            pltpu.VMEM((4, 2, 8, K), F32),
            pltpu.VMEM((8, C), F32),
            pltpu.VMEM((8, C), F32),
            pltpu.VMEM((K, C), F32),
            pltpu.VMEM((K, C), F32),
            pltpu.VMEM((2 * K, C), BF16),
            pltpu.VMEM((2 * K, C), BF16),
            pltpu.VMEM((4, 2, 8, K), F32),
            pltpu.VMEM((8, C), F32),
            pltpu.VMEM((8, C), F32),
            pltpu.VMEM((2, 4, 8, K), F32),
            pltpu.VMEM((8, 2, 4, 8, K), F32),
            pltpu.VMEM((512, 2 * K), BF16),
            pltpu.VMEM((8, 4, 8, C), F32),
            pltpu.VMEM((2, 4, 4, 8, WA), F32),
            pltpu.VMEM((3, 8, WA), F32),
            pltpu.VMEM((3, 8, 8, WB), F32),
            pltpu.VMEM((7, 8, WB), F32),
            pltpu.VMEM((8, 4, 8, C), F32),
            pltpu.VMEM((8, 32, 2 * K), F32),
            pltpu.VMEM((2, 3, 32, 2 * K), F32),
            pltpu.VMEM((2, 2, 32, K), F32),
            pltpu.VMEM((3, 32, K), F32),
            dma((7,)),
            dma((SB + 11,)),
            dma,
            dma((8, 2, 2)),
            dma((2, 2, 4, 4)),
            dma((2, 3)),
            dma((2, 3)),
            dma((7,)),
            dma((2, 2, 4, 4)),
            dma((2, 3)),
            dma((7,)),
            dma((8, 3)),
            dma((2, 3)),
            dma((3,)),
        ],
        compiler_params=pltpu.CompilerParams(
            collective_id=0, has_side_effects=True, vmem_limit_bytes=58 * 2**20
        ),
        name="soap_step",
    )(grad.reshape(4, 2, 8, K), basis, m1, m2)
    update, nf, ns = pl.pallas_call(
        hand_over,
        out_shape=tuple(jax.ShapeDtypeStruct(a.shape, F32) for a in (update, nf, ns)),
        name="hand_over",
    )(update, nf, ns)
    return update.reshape(64, K), nf, ns


def solution(mesh):
    return jax.shard_map(
        shards,
        mesh=mesh,
        in_specs=(
            P("tensor", "fsdp"),
            P("fsdp", "tensor"),
            P("fsdp", "tensor"),
            P("fsdp", "tensor"),
        ),
        out_specs=(P("tensor", "fsdp"), P("fsdp", "tensor"), P("fsdp", "tensor")),
        check_vma=False,
    )
```

```python
import jax
import jax.numpy as jnp
from jax import lax
from jax.experimental import pallas as pl
from jax.experimental.pallas import tpu as pltpu
from jax.sharding import PartitionSpec as P

MESH = pl.DeviceIdType.MESH
F32, BF16 = jnp.float32, jnp.bfloat16
STEP = 10
C = 2048
K = 256
PARTS = ((0, 1024), (1024, 512))
WA = PARTS[1][0] + PARTS[1][1]
WB = C - WA
FAR = (4, 3, -3, 2, -2, 1, -1)
SB = 200


def moment_step(rotated, first_moment, second_moment):
    new_first = 0.9 * first_moment + 0.1 * rotated
    new_second = 0.95 * second_moment + 0.05 * rotated * rotated
    first_fix = 1.0 - 0.9**STEP
    second_fix = 1.0 - 0.95**STEP
    direction = new_first / first_fix / (jnp.sqrt(new_second / second_fix) + 1e-08)
    return (new_first, new_second, direction)


def halves(x):
    hi = x.astype(BF16)
    return hi, (x - hi.astype(F32)).astype(BF16)


def kernel(
    grad_hbm, basis, m1_hbm, m2_hbm,
    update_hbm, nf_hbm, ns_hbm,
    update, nf, ns, own, sib, bhi, blo, grad, m1, m2, gl, g, ast, pf, ra, ya, yb, rb, d, u, xr, st, fin,
    local_sem, send, basis_sem, g_sem, ra_sem, ya_sem, yb_sem, rb_sem,
    da_sem, dya_sem, db_sem, dyb_sem, x_sem, fin_sem,
):
    f, t = lax.axis_index("fsdp"), lax.axis_index("tensor")
    z, yl, c = f // 8, (f // 2) % 4, f % 2
    yh, x = t // 4, t % 4

    def dev(dx=0, dh=0, dl=0, dz=0, dc=0):
        return (
            ((z + dz + 8) % 8) * 8 + ((yl + dl + 4) % 4) * 2 + (c + dc) % 2,
            ((yh + dh) % 2) * 4 + (x + dx + 4) % 4,
        )

    barrier = pltpu.get_barrier_semaphore()
    friends = [dev(dh=1, dc=e) for e in (0, 1)]
    friends += [dev(dx=j, dc=e) for j in (2, 1, 3) for e in (0, 1)]
    friends += [dev(dl=j) for j in (1, 2, 3)]
    friends += [dev(dz=k) for k in FAR] + [dev(dc=1)]
    for friend in friends:
        pl.semaphore_signal(barrier, inc=1, device_id=friend, device_id_type=MESH)
    loads = [
        pltpu.make_async_copy(a, b, local_sem.at[i])
        for i, (a, b) in enumerate(
            ((grad_hbm, grad), (basis, own), (m1_hbm, m1), (m2_hbm, m2))
        )
    ]
    for copy in loads:
        copy.start()
    outs = [
        pltpu.make_async_copy(a, b, local_sem.at[4 + i])
        for i, (a, b) in enumerate(((update, update_hbm), (nf, nf_hbm), (ns, ns_hbm)))
    ]

    started = []

    def put(src, dst, recv_sem, to):
        copy = pltpu.make_async_remote_copy(
            src_ref=src, dst_ref=dst, send_sem=send.at[len(started)],
            recv_sem=recv_sem, device_id=to, device_id_type=MESH,
        )
        copy.start()
        started.append(copy)

    def got(dst, recv_sem):
        pltpu.make_async_remote_copy(
            src_ref=dst, dst_ref=dst, send_sem=send.at[0],
            recv_sem=recv_sem, device_id=dev(dc=1), device_id_type=MESH,
        ).wait_recv()

    def split_basis(src, base):
        @pl.loop(0, K // 16)
        def _(i):
            hi, lo = halves(src[pl.ds(pl.multiple_of(i * 16, 16), 16), :])
            at = pl.multiple_of(base + i * 16, 16)
            bhi[pl.ds(at, 16), :] = hi
            blo[pl.ds(at, 16), :] = lo

    loads[0].wait()
    for e in (0, 1):
        for j in range(4):
            gl[e, j] = grad[(yl + j) % 4, (c + e) % 2]
    g[t, 0] = gl[0]
    pl.semaphore_wait(barrier, len(friends))

    tp = ((yh + 1) % 2) * 4 + x
    HALF = (pl.ds(0, 2), pl.ds(2, 2))
    for h in (0, 1):
        for e in (0, 1):
            put(gl.at[e, HALF[h]], g.at[t, e, HALF[h]], g_sem.at[1, e, h], dev(dh=1, dc=e))
    for j in (1, 3, 2):
        for e in (0, 1):
            put(gl.at[e], g.at[t, e], g_sem.at[1 + j, e, 0], dev(dx=j, dc=e))
    put(gl.at[1], g.at[t, 1], g_sem.at[0, 1, 0], dev(dc=1))
    put(basis, sib, basis_sem, dev(dc=1))
    loads[1].wait()
    split_basis(own, 0)
    for h in (0, 1):
        for e in (0, 1):
            got(g.at[tp, e, HALF[h]], g_sem.at[1, e, h])
        for j in (1, 3, 2):
            put(
                g.at[tp, :, HALF[h]], g.at[tp, :, HALF[h]],
                g_sem.at[4 + j, 0, h], dev(dx=j),
            )
    got(sib, basis_sem)
    split_basis(sib, K)
    got(g.at[t, 1], g_sem.at[0, 1, 0])
    for j in (1, 3, 2):
        for e in (0, 1):
            got(g.at[yh * 4 + (x + 4 - j) % 4, e], g_sem.at[1 + j, e, 0])

    def split_grad(side):
        first = pl.multiple_of(side * 128, 128)
        for e in (0, 1):
            hi, lo = halves(g[pl.ds(side * 4, 4), e].reshape(128, K))
            ast[pl.ds(first, 128), e * K : (e + 1) * K] = hi
            ast[pl.ds(256 + first, 128), e * K : (e + 1) * K] = lo

    def front(base, width, side=None):
        for at in range(base, base + width, 256):
            step = min(256, base + width - at)
            cols = pl.ds(at, step)
            if side is None:
                hi, both, rows, blocks = ast[0:256, :], ast[...], 256, pl.ds(0, 8)
            else:
                first = pl.multiple_of(side * 128, 128)
                hi = ast[pl.ds(first, 128), :]
                both = jnp.concatenate([hi, ast[pl.ds(256 + first, 128), :]], 0)
                rows, blocks = 128, pl.ds(side * 4, 4)
            big = jnp.dot(both, bhi[:, cols], preferred_element_type=F32)
            out = big[0:rows] + big[rows : 2 * rows]
            out += jnp.dot(hi, blo[:, cols], preferred_element_type=F32)
            pf[blocks, :, :, cols] = out.reshape(rows // 32, 4, 8, step)

    acols = [pl.ds(*PARTS[a]) for a in (0, 1)]
    bcols = pl.ds(WA, WB)

    def front_b(side, n):
        front(WA, WB, side)
        blocks = pl.ds(side * 4, 4)
        for j in (1, 2, 3):
            put(
                pf.at[blocks, j, :, bcols], yb.at[j - 1, blocks],
                yb_sem.at[n, j - 1], dev(dl=j),
            )

    split_grad(yh)
    front_b(yh, 0)
    for part in PARTS:
        front(*part, yh)
    for h in (0, 1):
        for j in (1, 3, 2):
            got(
                g.at[((yh + 1) % 2) * 4 + (x + 4 - j) % 4, :, HALF[h]],
                g_sem.at[4 + j, 0, h],
            )
    split_grad((yh + 1) % 2)

    SIGN = (1, -1)

    def zed(k):
        return (z + k + 16) % 8

    def send_a(a, s, j, way):
        put(
            pf.at[zed(SIGN[way] * (4 - s)), j, :, acols[a]],
            ra.at[way, s, j, :, acols[a]],
            ra_sem.at[way, a, s, j], dev(dz=SIGN[way]),
        )

    def add_a(a, s, j, way):
        piece = ra.at[way, s, j, :, acols[a]]
        got(piece, ra_sem.at[way, a, s, j])
        at = zed(SIGN[way] * (3 - s))
        pf[at, j, :, acols[a]] = pf[at, j, :, acols[a]] + piece[...]

    def round_a(a, r):
        for j in (2, 3, 1, 0):
            for way in (0, 1):
                s = r if (j >= 2) == (way == 0) else r + 1
                if s >= 1 and r >= 1 and s <= 4:
                    add_a(a, s - 1, j, way)
                if s <= 3:
                    send_a(a, s, j, way)
            if r == 4 and j:
                put(
                    pf.at[z, j, :, acols[a]], ya.at[j - 1, :, acols[a]],
                    ya_sem.at[a, j - 1], dev(dl=j),
                )

    def begin_b():
        for n, side in enumerate((yh, (yh + 1) % 2)):
            for j in (1, 2, 3):
                got(yb.at[j - 1, pl.ds(side * 4, 4)], yb_sem.at[n, j - 1])
        pf[:, 0, :, bcols] = pf[:, 0, :, bcols] + yb[0] + yb[1] + yb[2]
        for i, k in enumerate(FAR):
            put(pf.at[zed(k), 0, :, bcols], rb.at[i], rb_sem.at[i], dev(dz=k))

    def end_b():
        total = pf[z, 0, :, bcols]
        for i in range(7):
            got(rb.at[i], rb_sem.at[i])
            total = total + rb[i]
        moments(total, bcols)
        block = d.at[z, 0, :, bcols]
        for i, k in enumerate(FAR):
            put(block, block, db_sem.at[i], dev(dz=k))
        spread_b(0)

    def moments(rotated, cols):
        a, b, direction = moment_step(rotated, m1[:, cols], m2[:, cols])
        nf[:, cols] = a
        ns[:, cols] = b
        d[z, 0, :, cols] = direction

    def fwd_a(a, s, j):
        for way in (0, 1):
            at = zed(-SIGN[way] * s)
            block = d.at[at, j, :, acols[a]]
            if s:
                got(block, da_sem.at[way, a, s - 1, j])
            if s < 3 or (j < 2) == (way == 0):
                put(block, block, da_sem.at[way, a, s, j], dev(dz=SIGN[way]))

    def begin_a(a):
        for j in (1, 2, 3):
            got(ya.at[j - 1, :, acols[a]], ya_sem.at[a, j - 1])
        moments(
            pf[z, 0, :, acols[a]] + ya[0, :, acols[a]] + ya[1, :, acols[a]]
            + ya[2, :, acols[a]], acols[a],
        )
        for j in (1, 2, 3):
            put(
                d.at[z, 0, :, acols[a]], d.at[z, 4 - j, :, acols[a]],
                dya_sem.at[a, j - 1], dev(dl=j),
            )
        fwd_a(a, 0, 0)

    def gather_a(a, s):
        if s:
            fwd_a(a, s, 0)
        for j in (3, 1, 2):
            if s == 0:
                got(d.at[z, j, :, acols[a]], dya_sem.at[a, 3 - j])
            fwd_a(a, s, j)

    def end_a(a):
        for j in range(4):
            got(d.at[zed(4), j, :, acols[a]], da_sem.at[j // 2, a, 3, j])

    def spread_b(k):
        for j in (1, 2, 3):
            put(
                d.at[zed(k), 0, :, bcols], d.at[zed(k), 4 - j, :, bcols],
                dyb_sem.at[k % 8, j - 1], dev(dl=j),
            )

    def gather_b(*ks):
        for k in ks:
            got(d.at[zed(k), 0, :, bcols], db_sem.at[FAR.index(4 if k == 4 else -k)])
            spread_b(k)

    def wait_b(*ks):
        for k in ks:
            for j in (1, 2, 3):
                got(d.at[zed(k), 4 - j, :, bcols], dyb_sem.at[k % 8, j - 1])

    NT = (((1,), (1,)), ((), ()))

    cond_sends = []

    def back(part, ks):
        first, width = (PARTS[0], (PARTS[0][1], C - PARTS[0][1]), (WA, WB), PARTS[1])[part]
        cols = pl.ds(first, width)
        rows = 32 * len(ks)
        parts = [d[zed(k), :, :, cols].reshape(32, width) for k in ks]
        hi, lo = halves(jnp.concatenate(parts, 0) if len(ks) > 1 else parts[0])
        both = jnp.concatenate([hi, lo], 0)
        for e in (1, 0):
            at = pl.ds(e * K, K)
            big = lax.dot_general(both, bhi[at, cols], NT, preferred_element_type=F32)
            out = big[0:rows] + big[rows : 2 * rows]
            out += lax.dot_general(hi, blo[at, cols], NT, preferred_element_type=F32)
            for i, k in enumerate(ks):
                mine = out[32 * i : 32 * i + 32]
                u[zed(k), e] = u[zed(k), e] + mine if part else mine
            if part in (0, 2):
                continue
            for k in ks:
                tt = zed(k)
                xx, hh = tt % 4, tt // 4
                slot = jnp.minimum((xx + 7 - x) % 4, 2)
                copy = pltpu.make_async_remote_copy(
                    src_ref=u.at[tt, e], dst_ref=xr.at[hh, slot, e],
                    send_sem=send.at[SB + len(cond_sends)],
                    recv_sem=x_sem.at[hh, slot, e],
                    device_id=(f, yh * 4 + xx), device_id_type=MESH,
                )
                cond_sends.append((copy, xx != x))

                @pl.when(xx != x)
                def _():
                    copy.start()

    other = (yh + 1) % 2

    def final_copy(i, src, to):
        return pltpu.make_async_remote_copy(
            src_ref=src, dst_ref=fin.at[i], send_sem=send.at[SB + 16 + i],
            recv_sem=fin_sem.at[i], device_id=to, device_id_type=MESH,
        )

    final = [
        final_copy(0, st.at[yh, 1], dev(dc=1)),
        final_copy(1, st.at[other, 0], dev(dh=1)),
        final_copy(2, st.at[other, 1], dev(dh=1, dc=1)),
    ]

    def finish(k):
        tt = zed(k)
        hh = tt // 4

        @pl.when(tt % 4 == x)
        def _():
            for e in (1, 0):
                for j in (1, 3, 2):
                    got(xr.at[hh, j - 1, e], x_sem.at[hh, j - 1, e])
                st[hh, e] = u[tt, e] + xr[hh, 0, e] + xr[hh, 1, e] + xr[hh, 2, e]
                if e:

                    @pl.when(hh == yh)
                    def _():
                        final[0].start()

                @pl.when(hh != yh)
                def _():
                    final[1 + e].start()

    late = (yh + 1) % 2
    front(*PARTS[0], late)
    round_a(0, 0)
    front_b(late, 1)
    front(*PARTS[1], late)
    round_a(1, 0)
    for copy in loads[2:]:
        copy.wait()
    round_a(0, 1)
    round_a(1, 1)
    round_a(0, 2)
    round_a(1, 2)
    round_a(0, 3)
    round_a(1, 3)
    begin_b()
    round_a(0, 4)
    round_a(1, 4)
    begin_a(0)
    begin_a(1)
    end_b()
    gather_a(0,0)
    gather_a(1,0)
    gather_a(0,1)
    gather_b(1,-1)
    gather_b(2,-2)
    gather_a(1,1)
    gather_b(3,-3)
    gather_b(4)
    back(0,[0])
    back(0,[1,-1])
    outs[1].start()
    outs[2].start()
    gather_a(0,2)
    wait_b(0)
    back(1,[0])
    gather_a(1,2)
    back(0,[2,-2])
    wait_b(1,-1)
    back(1,[1,-1])
    gather_a(0, 3)
    gather_a(1, 3)
    finish(0)
    back(0, [3, -3])
    wait_b(2, -2)
    back(1, [2, -2])
    finish(1)
    finish(-1)
    end_a(0)
    back(0, [4])
    wait_b(3, -3)
    back(1, [3, -3])
    finish(2)
    finish(-2)
    wait_b(4)
    back(2, [4])
    end_a(1)
    back(3, [4])
    finish(3)
    finish(-3)
    finish(4)

    for i in range(3):
        got(fin.at[i], fin_sem.at[i])
    mine = st[yh, 0] + fin[1]
    theirs = fin[0] + fin[2]
    for j in range(4):
        update[(yl + j) % 4, c] = mine[8 * j : 8 * j + 8]
        update[(yl + j) % 4, 1 - c] = theirs[8 * j : 8 * j + 8]

    assert len(started) <= SB
    outs[0].start()
    for copy in started:
        copy.wait_send()
    for copy, pred in cond_sends:
        @pl.when(pred)
        def _():
            copy.wait_send()
    for copy in final:
        copy.wait_send()
    for copy in outs:
        copy.wait()


def hand_over(a, b, c, to_a, to_b, to_c):
    to_a[...] = a[...]
    to_b[...] = b[...]
    to_c[...] = c[...]


def shards(grad, basis, m1, m2):
    anywhere = pl.BlockSpec(memory_space=pl.ANY)
    dma = pltpu.SemaphoreType.DMA
    update, nf, ns = pl.pallas_call(
        kernel,
        out_shape=(
            jax.ShapeDtypeStruct((4, 2, 8, K), F32),
            jax.ShapeDtypeStruct((8, C), F32),
            jax.ShapeDtypeStruct((8, C), F32),
        ),
        in_specs=[anywhere] * 4,
        out_specs=(anywhere,) * 3,
        scratch_shapes=[
            pltpu.VMEM((4, 2, 8, K), F32),
            pltpu.VMEM((8, C), F32),
            pltpu.VMEM((8, C), F32),
            pltpu.VMEM((K, C), F32),
            pltpu.VMEM((K, C), F32),
            pltpu.VMEM((2 * K, C), BF16),
            pltpu.VMEM((2 * K, C), BF16),
            pltpu.VMEM((4, 2, 8, K), F32),
            pltpu.VMEM((8, C), F32),
            pltpu.VMEM((8, C), F32),
            pltpu.VMEM((2, 4, 8, K), F32),
            pltpu.VMEM((8, 2, 4, 8, K), F32),
            pltpu.VMEM((512, 2 * K), BF16),
            pltpu.VMEM((8, 4, 8, C), F32),
            pltpu.VMEM((2, 4, 4, 8, WA), F32),
            pltpu.VMEM((3, 8, WA), F32),
            pltpu.VMEM((3, 8, 8, WB), F32),
            pltpu.VMEM((7, 8, WB), F32),
            pltpu.VMEM((8, 4, 8, C), F32),
            pltpu.VMEM((8, 2, 32, K), F32),
            pltpu.VMEM((2, 3, 2, 32, K), F32),
            pltpu.VMEM((2, 2, 32, K), F32),
            pltpu.VMEM((3, 32, K), F32),
            dma((7,)),
            dma((SB + 19,)),
            dma,
            dma((8, 2, 2)),
            dma((2, 2, 4, 4)),
            dma((2, 3)),
            dma((2, 3)),
            dma((7,)),
            dma((2, 2, 4, 4)),
            dma((2, 3)),
            dma((7,)),
            dma((8, 3)),
            dma((2, 3, 2)),
            dma((3,)),
        ],
        compiler_params=pltpu.CompilerParams(
            collective_id=0, has_side_effects=True, vmem_limit_bytes=58 * 2**20
        ),
        name="soap_step",
    )(grad.reshape(4, 2, 8, K), basis, m1, m2)
    update, nf, ns = pl.pallas_call(
        hand_over,
        out_shape=tuple(jax.ShapeDtypeStruct(a.shape, F32) for a in (update, nf, ns)),
        name="hand_over",
    )(update, nf, ns)
    return update.reshape(64, K), nf, ns


def solution(mesh):
    return jax.shard_map(
        shards,
        mesh=mesh,
        in_specs=(
            P("tensor", "fsdp"),
            P("fsdp", "tensor"),
            P("fsdp", "tensor"),
            P("fsdp", "tensor"),
        ),
        out_specs=(P("tensor", "fsdp"), P("fsdp", "tensor"), P("fsdp", "tensor")),
        check_vma=False,
    )
```

```python
import jax
import jax.numpy as jnp
from jax import lax
from jax.experimental import pallas as pl
from jax.experimental.pallas import tpu as pltpu
from jax.sharding import PartitionSpec as P

MESH = pl.DeviceIdType.MESH
F32, BF16 = jnp.float32, jnp.bfloat16
STEP = 10
C = 2048
K = 256
PARTS = ((0, 1024), (1024, 512))
WA = PARTS[1][0] + PARTS[1][1]
WB = C - WA
FAR = (4, 3, -3, 2, -2, 1, -1)
SB = 200


def moment_step(rotated, first_moment, second_moment):
    new_first = 0.9 * first_moment + 0.1 * rotated
    new_second = 0.95 * second_moment + 0.05 * rotated * rotated
    first_fix = 1.0 - 0.9**STEP
    second_fix = 1.0 - 0.95**STEP
    direction = new_first / first_fix / (jnp.sqrt(new_second / second_fix) + 1e-08)
    return (new_first, new_second, direction)


def halves(x):
    hi = x.astype(BF16)
    return hi, (x - hi.astype(F32)).astype(BF16)


def kernel(
    grad_hbm, basis, m1_hbm, m2_hbm,
    update_hbm, nf_hbm, ns_hbm,
    update, nf, ns, own, sib, bhi, blo, grad, m1, m2, gl, g, ast, pf, ra, ya, yb, rb, d, u, xr, st, fin,
    local_sem, send, basis_sem, g_sem, ra_sem, ya_sem, yb_sem, rb_sem,
    da_sem, dya_sem, db_sem, dyb_sem, x_sem, fin_sem,
):
    f, t = lax.axis_index("fsdp"), lax.axis_index("tensor")
    z, yl, c = f // 8, (f // 2) % 4, f % 2
    yh, x = t // 4, t % 4

    def dev(dx=0, dh=0, dl=0, dz=0, dc=0):
        return (
            ((z + dz + 8) % 8) * 8 + ((yl + dl + 4) % 4) * 2 + (c + dc) % 2,
            ((yh + dh) % 2) * 4 + (x + dx + 4) % 4,
        )

    barrier = pltpu.get_barrier_semaphore()
    friends = [dev(dh=1, dc=e) for e in (0, 1)]
    friends += [dev(dx=j, dc=e) for j in (2, 1, 3) for e in (0, 1)]
    friends += [dev(dl=j) for j in (1, 2, 3)]
    friends += [dev(dz=k) for k in FAR] + [dev(dc=1)]
    for friend in friends:
        pl.semaphore_signal(barrier, inc=1, device_id=friend, device_id_type=MESH)
    loads = [
        pltpu.make_async_copy(a, b, local_sem.at[i])
        for i, (a, b) in enumerate(
            ((grad_hbm, grad), (basis, own), (m1_hbm, m1), (m2_hbm, m2))
        )
    ]
    for copy in loads:
        copy.start()
    outs = [
        pltpu.make_async_copy(a, b, local_sem.at[4 + i])
        for i, (a, b) in enumerate(((update, update_hbm), (nf, nf_hbm), (ns, ns_hbm)))
    ]

    started = []

    def put(src, dst, recv_sem, to):
        copy = pltpu.make_async_remote_copy(
            src_ref=src, dst_ref=dst, send_sem=send.at[len(started)],
            recv_sem=recv_sem, device_id=to, device_id_type=MESH,
        )
        copy.start()
        started.append(copy)

    def got(dst, recv_sem):
        pltpu.make_async_remote_copy(
            src_ref=dst, dst_ref=dst, send_sem=send.at[0],
            recv_sem=recv_sem, device_id=dev(dc=1), device_id_type=MESH,
        ).wait_recv()

    def split_basis(src, base):
        @pl.loop(0, K // 16)
        def _(i):
            hi, lo = halves(src[pl.ds(pl.multiple_of(i * 16, 16), 16), :])
            at = pl.multiple_of(base + i * 16, 16)
            bhi[pl.ds(at, 16), :] = hi
            blo[pl.ds(at, 16), :] = lo

    loads[0].wait()
    for e in (0, 1):
        for j in range(4):
            gl[e, j] = grad[(yl + j) % 4, (c + e) % 2]
    g[t, 0] = gl[0]
    pl.semaphore_wait(barrier, len(friends))

    tp = ((yh + 1) % 2) * 4 + x
    HALF = (pl.ds(0, 2), pl.ds(2, 2))
    for h in (0, 1):
        for e in (0, 1):
            put(gl.at[e, HALF[h]], g.at[t, e, HALF[h]], g_sem.at[1, e, h], dev(dh=1, dc=e))
    for j in (1, 3, 2):
        for e in (0, 1):
            put(gl.at[e], g.at[t, e], g_sem.at[1 + j, e, 0], dev(dx=j, dc=e))
    put(gl.at[1], g.at[t, 1], g_sem.at[0, 1, 0], dev(dc=1))
    put(basis, sib, basis_sem, dev(dc=1))
    loads[1].wait()
    split_basis(own, 0)
    for h in (0, 1):
        for e in (0, 1):
            got(g.at[tp, e, HALF[h]], g_sem.at[1, e, h])
        for j in (1, 3, 2):
            put(
                g.at[tp, :, HALF[h]], g.at[tp, :, HALF[h]],
                g_sem.at[4 + j, 0, h], dev(dx=j),
            )
    got(sib, basis_sem)
    split_basis(sib, K)
    got(g.at[t, 1], g_sem.at[0, 1, 0])
    for j in (1, 3, 2):
        for e in (0, 1):
            got(g.at[yh * 4 + (x + 4 - j) % 4, e], g_sem.at[1 + j, e, 0])

    def split_grad(side):
        first = pl.multiple_of(side * 128, 128)
        for e in (0, 1):
            hi, lo = halves(g[pl.ds(side * 4, 4), e].reshape(128, K))
            ast[pl.ds(first, 128), e * K : (e + 1) * K] = hi
            ast[pl.ds(256 + first, 128), e * K : (e + 1) * K] = lo

    def front(base, width, side=None):
        for at in range(base, base + width, 256):
            step = min(256, base + width - at)
            cols = pl.ds(at, step)
            if side is None:
                hi, both, rows, blocks = ast[0:256, :], ast[...], 256, pl.ds(0, 8)
            else:
                first = pl.multiple_of(side * 128, 128)
                hi = ast[pl.ds(first, 128), :]
                both = jnp.concatenate([hi, ast[pl.ds(256 + first, 128), :]], 0)
                rows, blocks = 128, pl.ds(side * 4, 4)
            big = jnp.dot(both, bhi[:, cols], preferred_element_type=F32)
            out = big[0:rows] + big[rows : 2 * rows]
            out += jnp.dot(hi, blo[:, cols], preferred_element_type=F32)
            pf[blocks, :, :, cols] = out.reshape(rows // 32, 4, 8, step)

    acols = [pl.ds(*PARTS[a]) for a in (0, 1)]
    bcols = pl.ds(WA, WB)

    def front_b(side, n):
        front(WA, WB, side)
        blocks = pl.ds(side * 4, 4)
        for j in (1, 2, 3):
            put(
                pf.at[blocks, j, :, bcols], yb.at[j - 1, blocks],
                yb_sem.at[n, j - 1], dev(dl=j),
            )

    split_grad(yh)
    front_b(yh, 0)
    for part in PARTS:
        front(*part, yh)
    for h in (0, 1):
        for j in (1, 3, 2):
            got(
                g.at[((yh + 1) % 2) * 4 + (x + 4 - j) % 4, :, HALF[h]],
                g_sem.at[4 + j, 0, h],
            )
    split_grad((yh + 1) % 2)

    SIGN = (1, -1)

    def zed(k):
        return (z + k + 16) % 8

    def send_a(a, s, j, way):
        put(
            pf.at[zed(SIGN[way] * (4 - s)), j, :, acols[a]],
            ra.at[way, s, j, :, acols[a]],
            ra_sem.at[way, a, s, j], dev(dz=SIGN[way]),
        )

    def add_a(a, s, j, way):
        piece = ra.at[way, s, j, :, acols[a]]
        got(piece, ra_sem.at[way, a, s, j])
        at = zed(SIGN[way] * (3 - s))
        pf[at, j, :, acols[a]] = pf[at, j, :, acols[a]] + piece[...]

    def round_a(a, r):
        for j in (2, 3, 1, 0):
            for way in (0, 1):
                s = r if (j >= 2) == (way == 0) else r + 1
                if s >= 1 and r >= 1 and s <= 4:
                    add_a(a, s - 1, j, way)
                if s <= 3:
                    send_a(a, s, j, way)
            if r == 4 and j:
                put(
                    pf.at[z, j, :, acols[a]], ya.at[j - 1, :, acols[a]],
                    ya_sem.at[a, j - 1], dev(dl=j),
                )

    def begin_b():
        for n, side in enumerate((yh, (yh + 1) % 2)):
            for j in (1, 2, 3):
                got(yb.at[j - 1, pl.ds(side * 4, 4)], yb_sem.at[n, j - 1])
        pf[:, 0, :, bcols] = pf[:, 0, :, bcols] + yb[0] + yb[1] + yb[2]
        for i, k in enumerate(FAR):
            put(pf.at[zed(k), 0, :, bcols], rb.at[i], rb_sem.at[i], dev(dz=k))

    def end_b():
        total = pf[z, 0, :, bcols]
        for i in range(7):
            got(rb.at[i], rb_sem.at[i])
            total = total + rb[i]
        moments(total, bcols)
        block = d.at[z, 0, :, bcols]
        for i, k in enumerate(FAR):
            put(block, block, db_sem.at[i], dev(dz=k))
        spread_b(0)

    def moments(rotated, cols):
        a, b, direction = moment_step(rotated, m1[:, cols], m2[:, cols])
        nf[:, cols] = a
        ns[:, cols] = b
        d[z, 0, :, cols] = direction

    def fwd_a(a, s, j):
        for way in (0, 1):
            at = zed(-SIGN[way] * s)
            block = d.at[at, j, :, acols[a]]
            if s:
                got(block, da_sem.at[way, a, s - 1, j])
            if s < 3 or (j < 2) == (way == 0):
                put(block, block, da_sem.at[way, a, s, j], dev(dz=SIGN[way]))

    def begin_a(a):
        for j in (1, 2, 3):
            got(ya.at[j - 1, :, acols[a]], ya_sem.at[a, j - 1])
        moments(
            pf[z, 0, :, acols[a]] + ya[0, :, acols[a]] + ya[1, :, acols[a]]
            + ya[2, :, acols[a]], acols[a],
        )
        for j in (1, 2, 3):
            put(
                d.at[z, 0, :, acols[a]], d.at[z, 4 - j, :, acols[a]],
                dya_sem.at[a, j - 1], dev(dl=j),
            )
        fwd_a(a, 0, 0)

    def gather_a(a, s):
        if s:
            fwd_a(a, s, 0)
        for j in (3, 1, 2):
            if s == 0:
                got(d.at[z, j, :, acols[a]], dya_sem.at[a, 3 - j])
            fwd_a(a, s, j)

    def end_a(a):
        for j in range(4):
            got(d.at[zed(4), j, :, acols[a]], da_sem.at[j // 2, a, 3, j])

    def spread_b(k):
        for j in (1, 2, 3):
            put(
                d.at[zed(k), 0, :, bcols], d.at[zed(k), 4 - j, :, bcols],
                dyb_sem.at[k % 8, j - 1], dev(dl=j),
            )

    def gather_b(*ks):
        for k in ks:
            got(d.at[zed(k), 0, :, bcols], db_sem.at[FAR.index(4 if k == 4 else -k)])
            spread_b(k)

    def wait_b(*ks):
        for k in ks:
            for j in (1, 2, 3):
                got(d.at[zed(k), 4 - j, :, bcols], dyb_sem.at[k % 8, j - 1])

    NT = (((1,), (1,)), ((), ()))

    cond_sends = []

    def back(part, ks):
        first, width = (PARTS[0], (PARTS[0][1], C - PARTS[0][1]), (WA, WB), PARTS[1])[part]
        cols = pl.ds(first, width)
        rows = 32 * len(ks)
        parts = [d[zed(k), :, :, cols].reshape(32, width) for k in ks]
        hi, lo = halves(jnp.concatenate(parts, 0) if len(ks) > 1 else parts[0])
        both = jnp.concatenate([hi, lo], 0)
        for e in (1, 0):
            at = pl.ds(e * K, K)
            big = lax.dot_general(both, bhi[at, cols], NT, preferred_element_type=F32)
            out = big[0:rows] + big[rows : 2 * rows]
            out += lax.dot_general(hi, blo[at, cols], NT, preferred_element_type=F32)
            for i, k in enumerate(ks):
                mine = out[32 * i : 32 * i + 32]
                u[zed(k), e] = u[zed(k), e] + mine if part else mine
            if part in (0, 2):
                continue
            for k in ks:
                tt = zed(k)
                xx, hh = tt % 4, tt // 4
                slot = jnp.minimum((xx + 7 - x) % 4, 2)
                copy = pltpu.make_async_remote_copy(
                    src_ref=u.at[tt, e], dst_ref=xr.at[hh, slot, e],
                    send_sem=send.at[SB + len(cond_sends)],
                    recv_sem=x_sem.at[hh, slot, e],
                    device_id=(f, yh * 4 + xx), device_id_type=MESH,
                )
                cond_sends.append((copy, xx != x))

                @pl.when(xx != x)
                def _():
                    copy.start()

    other = (yh + 1) % 2

    def final_copy(i, src, to):
        return pltpu.make_async_remote_copy(
            src_ref=src, dst_ref=fin.at[i], send_sem=send.at[SB + 16 + i],
            recv_sem=fin_sem.at[i], device_id=to, device_id_type=MESH,
        )

    final = [
        final_copy(0, st.at[yh, 1], dev(dc=1)),
        final_copy(1, st.at[other, 0], dev(dh=1)),
        final_copy(2, st.at[other, 1], dev(dh=1, dc=1)),
    ]

    def finish(k):
        tt = zed(k)
        hh = tt // 4

        @pl.when(tt % 4 == x)
        def _():
            for e in (1, 0):
                for j in (1, 3, 2):
                    got(xr.at[hh, j - 1, e], x_sem.at[hh, j - 1, e])
                st[hh, e] = u[tt, e] + xr[hh, 0, e] + xr[hh, 1, e] + xr[hh, 2, e]
                if e:

                    @pl.when(hh == yh)
                    def _():
                        final[0].start()

                @pl.when(hh != yh)
                def _():
                    final[1 + e].start()

    late = (yh + 1) % 2
    front(*PARTS[0], late)
    round_a(0, 0)
    front_b(late, 1)
    front(*PARTS[1], late)
    round_a(1, 0)
    for copy in loads[2:]:
        copy.wait()
    round_a(0, 1)
    round_a(1, 1)
    round_a(0, 2)
    round_a(1, 2)
    round_a(0, 3)
    round_a(1, 3)
    begin_b()
    round_a(0, 4)
    round_a(1, 4)
    begin_a(0)
    end_b()
    begin_a(1)
    gather_a(0, 0)
    gather_a(1, 0)
    back(0, [0])
    gather_a(0, 1)
    gather_b(1, -1)
    gather_b(2, -2)
    gather_a(1, 1)
    gather_b(3, -3)
    gather_b(4)
    back(0, [1, -1])
    outs[1].start()
    outs[2].start()
    gather_a(0, 2)
    wait_b(0)
    back(1, [0])
    back(0, [2, -2])
    gather_a(1, 2)
    wait_b(1, -1)
    back(1, [1, -1])
    gather_a(0, 3)
    back(0, [3, -3])
    wait_b(2, -2)
    back(1, [2, -2])
    gather_a(1, 3)
    finish(0)
    finish(1)
    finish(-1)
    end_a(0)
    back(0, [4])
    wait_b(3, -3)
    back(1, [3, -3])
    finish(2)
    finish(-2)
    wait_b(4)
    back(2, [4])
    end_a(1)
    back(3, [4])
    finish(3)
    finish(-3)
    finish(4)

    for i in range(3):
        got(fin.at[i], fin_sem.at[i])
    mine = st[yh, 0] + fin[1]
    theirs = fin[0] + fin[2]
    for j in range(4):
        update[(yl + j) % 4, c] = mine[8 * j : 8 * j + 8]
        update[(yl + j) % 4, 1 - c] = theirs[8 * j : 8 * j + 8]

    assert len(started) <= SB
    outs[0].start()
    for copy in started:
        copy.wait_send()
    for copy, pred in cond_sends:
        @pl.when(pred)
        def _():
            copy.wait_send()
    for copy in final:
        copy.wait_send()
    for copy in outs:
        copy.wait()


def hand_over(a, b, c, to_a, to_b, to_c):
    to_a[...] = a[...]
    to_b[...] = b[...]
    to_c[...] = c[...]


def shards(grad, basis, m1, m2):
    anywhere = pl.BlockSpec(memory_space=pl.ANY)
    dma = pltpu.SemaphoreType.DMA
    update, nf, ns = pl.pallas_call(
        kernel,
        out_shape=(
            jax.ShapeDtypeStruct((4, 2, 8, K), F32),
            jax.ShapeDtypeStruct((8, C), F32),
            jax.ShapeDtypeStruct((8, C), F32),
        ),
        in_specs=[anywhere] * 4,
        out_specs=(anywhere,) * 3,
        scratch_shapes=[
            pltpu.VMEM((4, 2, 8, K), F32),
            pltpu.VMEM((8, C), F32),
            pltpu.VMEM((8, C), F32),
            pltpu.VMEM((K, C), F32),
            pltpu.VMEM((K, C), F32),
            pltpu.VMEM((2 * K, C), BF16),
            pltpu.VMEM((2 * K, C), BF16),
            pltpu.VMEM((4, 2, 8, K), F32),
            pltpu.VMEM((8, C), F32),
            pltpu.VMEM((8, C), F32),
            pltpu.VMEM((2, 4, 8, K), F32),
            pltpu.VMEM((8, 2, 4, 8, K), F32),
            pltpu.VMEM((512, 2 * K), BF16),
            pltpu.VMEM((8, 4, 8, C), F32),
            pltpu.VMEM((2, 4, 4, 8, WA), F32),
            pltpu.VMEM((3, 8, WA), F32),
            pltpu.VMEM((3, 8, 8, WB), F32),
            pltpu.VMEM((7, 8, WB), F32),
            pltpu.VMEM((8, 4, 8, C), F32),
            pltpu.VMEM((8, 2, 32, K), F32),
            pltpu.VMEM((2, 3, 2, 32, K), F32),
            pltpu.VMEM((2, 2, 32, K), F32),
            pltpu.VMEM((3, 32, K), F32),
            dma((7,)),
            dma((SB + 19,)),
            dma,
            dma((8, 2, 2)),
            dma((2, 2, 4, 4)),
            dma((2, 3)),
            dma((2, 3)),
            dma((7,)),
            dma((2, 2, 4, 4)),
            dma((2, 3)),
            dma((7,)),
            dma((8, 3)),
            dma((2, 3, 2)),
            dma((3,)),
        ],
        compiler_params=pltpu.CompilerParams(
            collective_id=0, has_side_effects=True, vmem_limit_bytes=58 * 2**20
        ),
        name="soap_step",
    )(grad.reshape(4, 2, 8, K), basis, m1, m2)
    update, nf, ns = pl.pallas_call(
        hand_over,
        out_shape=tuple(jax.ShapeDtypeStruct(a.shape, F32) for a in (update, nf, ns)),
        name="hand_over",
    )(update, nf, ns)
    return update.reshape(64, K), nf, ns


def solution(mesh):
    return jax.shard_map(
        shards,
        mesh=mesh,
        in_specs=(
            P("tensor", "fsdp"),
            P("fsdp", "tensor"),
            P("fsdp", "tensor"),
            P("fsdp", "tensor"),
        ),
        out_specs=(P("tensor", "fsdp"), P("fsdp", "tensor"), P("fsdp", "tensor")),
        check_vma=False,
    )
```
